512 devices in a mesh: island: 8 (over x_lo, y), fsdp: 64 (over z, x_hi, core).
Axes of the slice: x: 4 (x_hi: 2, x_lo: 2; x = x_hi * 2 + x_lo), y: 4, z: 16, core: 2. Of those that a mesh axis runs over, the one named last changes fastest.
Arguments:
- activations: bfloat16 [131072, 8192], P(('island', 'fsdp')), may hold values from -24 to 24
- cotangent: bfloat16 [131072, 128], P(('island', 'fsdp')), may hold values from -0.0625 to 0.0625
- norm_gain: float32 [8, 8192], P('island'), may hold values from 0.5 to 1.5
- weight: bfloat16 [8, 8192, 128], P('island', 'fsdp'), may hold values from -0.0625 to 0.0625
- global_slab: float32 [64, 28672], P(None, 'fsdp'), may hold values from -6 to 6
- local_slab: bfloat16 [8, 64, 28672], P('island', None, 'fsdp'), may hold values from -6 to 6
- momentum: float32 [64, 28672], P(None, 'fsdp'), may hold values from -6 to 6
Outputs:
- values: bfloat16 [131072, 128], P(('island', 'fsdp'))
- weight_grad: float32 [8, 8192, 128], P('island', 'fsdp')
- gain_grad: float32 [8, 8192], P('island')
- new_global: float32 [64, 28672], P(None, 'fsdp')
- new_momentum: float32 [64, 28672], P(None, 'fsdp')
The draws below stay inside these ranges and needn't reach their ends.
All inputs are finite; a program needn't handle non-finite values.
Results may differ from the reference program's by a relative error of at most 0.02.
Values may be sent and summed in bfloat16 or wider, within the bound.
No kernel may reach another device: no remote copies, remote signals or barrier semaphores. Data moves between devices by JAX's collectives and lax.ppermute only.
A program may use at most 64 MiB of HBM per device.

```python
import jax
import jax.numpy as jnp
from jax import lax

D = 8192
FF = 28672
HD = 128
TOK_DEV = 256
SROWS = 64
ISLANDS = 8
TOKENS = 131072
N_ISLAND = 8
N_FSDP = 64


def raised(values, stream_key, source, target, shards_of, factor):
    owner, partner = [(jnp.arange(values.shape[dim]) // (values.shape[dim] // shards_of)).reshape([-1 if axis == dim else 1 for axis in range(values.ndim)]) for dim in (source, target)]
    chosen = jax.random.permutation(stream_key, shards_of)[partner]
    strong = (owner == chosen) | (owner == (partner + shards_of // 2) % shards_of)
    return jnp.where(strong, factor * values, values)


def shard_levels(rng, extent, pieces, least, largest):
    loudness = 1.0
    for axis_at, parts in pieces:
        draws = jax.random.uniform(jax.random.fold_in(jax.random.fold_in(rng, 6), axis_at), (parts,), jnp.float32, least / len(pieces), largest / len(pieces))
        loudness = loudness * jnp.repeat(jnp.exp(draws), extent[axis_at] // parts).reshape((-1,) + (1,) * (len(extent) - 1 - axis_at))
    return loudness


def centred(key, shape, spread, reach, shards=(), held_as=jnp.bfloat16):
    loudness = shard_levels(key, shape, shards, -0.22, 0.18) if shards else 1.0
    values = jax.random.normal(key, shape, jnp.float32) * spread * loudness
    return jnp.minimum(jnp.maximum(values, -reach), reach).astype(held_as)


def bell_draw_with(rng, shape, deviation, reach, pieces, heavy, kind=jnp.bfloat16):
    array = deviation * jax.random.normal(rng, shape, jnp.float32)
    if pieces:
        array = array * shard_levels(rng, shape, pieces, -0.22, 0.18)
    return jnp.clip(raised(array, jax.random.fold_in(rng, 3), *heavy), -reach, reach).astype(kind)


def setup_inputs(seed: int = 0) -> dict:
    streams_of = jax.random.split(jax.random.key(seed), 8)
    activations = bell_draw_with(streams_of[0], (TOKENS, D), 1.0, 24.0, ((0, 512),), (0, 1, 512, 6.0))
    cotangent = centred(streams_of[1], (TOKENS, HD), 0.01, 0.0625, ((0, 512),))
    norm_gain = jnp.clip(1.0 + 0.1 * jax.random.normal(streams_of[2], (ISLANDS, D), jnp.float32), 0.5, 1.5)
    weight = centred(streams_of[3], (ISLANDS, D, HD), D ** -0.5, 0.0625, ((0, 8), (1, 64)))
    global_slab = centred(streams_of[4], (SROWS, FF), 1.0, 6.0, ((1, 64),), jnp.float32)
    local_slab = centred(streams_of[5], (ISLANDS, SROWS, FF), 1.0, 6.0, ((0, 8), (2, 64)))
    momentum = centred(streams_of[6], (SROWS, FF), 1.0, 6.0, ((1, 64),), jnp.float32)
    return {"activations": activations, "cotangent": cotangent, "norm_gain": norm_gain, "weight": weight, "global_slab": global_slab, "local_slab": local_slab, "momentum": momentum}


def reference(activations, cotangent, norm_gain, weight, global_slab, local_slab, momentum):
    rows = TOK_DEV * N_FSDP
    value_list = []
    weight_list = []
    gain_list = []
    total = jnp.zeros(global_slab.shape, jnp.float32)
    for replica in range(N_ISLAND):
        tokens = activations[replica * rows:(replica + 1) * rows].astype(jnp.float32)
        inverse = lax.rsqrt(lax.optimization_barrier(jnp.mean(tokens * tokens, axis=1, keepdims=True)) + 1e-05)
        unit = tokens * inverse
        normed = (unit * norm_gain[replica][None, :]).astype(jnp.bfloat16)
        matrix = weight[replica]
        grads_out = cotangent[replica * rows:(replica + 1) * rows]
        value_list.append(jnp.dot(normed, matrix, preferred_element_type=jnp.float32).astype(jnp.bfloat16))
        weight_list.append(jnp.dot(normed.T, grads_out, preferred_element_type=jnp.float32))
        hidden_grad = jnp.dot(grads_out, matrix.T, preferred_element_type=jnp.float32)
        gain_list.append(lax.optimization_barrier(jnp.sum(hidden_grad * unit, axis=0)))
        delta = (global_slab - local_slab[replica].astype(jnp.float32)).astype(jnp.bfloat16)
        delta = lax.optimization_barrier(delta)
        total = total + delta.astype(jnp.float32)
    average = total / N_ISLAND
    new_momentum = 0.9 * momentum + average
    new_global = global_slab - 0.7 * (average + 0.9 * new_momentum)
    return (jnp.concatenate(value_list, axis=0), jnp.stack(weight_list), jnp.stack(gain_list), new_global, new_momentum)
```

```python
import jax
import jax.numpy as jnp
import numpy as np
from jax import lax
from jax.sharding import Mesh, PartitionSpec as P

Z, XH, CORE = 16, 2, 2
FSDP = ("z", "xh", "core")
f32, bf16 = jnp.float32, jnp.bfloat16


def swap(value, axis):
    return lax.ppermute(value, axis, [(0, 1), (1, 0)])


def to_all(value, axis, size):
    return lax.all_to_all(jnp.broadcast_to(value[None], (size,) + value.shape), axis, 0, 0)


def pair(mine, other, index, axis):
    first = jnp.where(index == 0, mine, other)
    second = jnp.where(index == 0, other, mine)
    return jnp.stack([first, second], axis=axis)


def shards(activations, cotangent, norm_gain, weight, global_slab, local_slab, momentum):
    xh, core = lax.axis_index("xh"), lax.axis_index("core")
    own = lambda a, i, axis: lax.dynamic_index_in_dim(a, i, axis, keepdims=False)
    gain = norm_gain.reshape(Z, XH, CORE, 128)
    gain_class = own(own(gain, core, 2), xh, 1)

    with jax.named_scope("weight_over_z"):
        weight_z = to_all(weight[0], "z", Z)

    with jax.named_scope("projection_grad"):
        tokens = activations.astype(f32)
        inverse = lax.rsqrt(jnp.mean(tokens * tokens, axis=1, keepdims=True) + 1e-05)
        scaled = (cotangent.astype(f32) * inverse).astype(bf16)
        grad = lax.dot_general(
            activations, scaled, (((0,), (0,)), ((), ())), preferred_element_type=f32
        ).astype(bf16)
        grad = grad.reshape(Z, XH, CORE, 128, 128)
        there = swap(own(grad, 1 - core, 2), "core")
        grad = own(grad, core, 2).astype(f32) + there.astype(f32)
        there = swap(own(grad, 1 - xh, 1).astype(bf16), "xh")
        grad = own(grad, xh, 1) + there.astype(f32)
        grad_own = jnp.sum(lax.all_to_all(grad.astype(bf16), "z", 0, 0).astype(f32), axis=0)

    with jax.named_scope("gain_grad"):
        part = jnp.sum(weight_z.astype(f32) * grad, axis=-1)
        part = jnp.sum(to_all(part, "z", Z), axis=0)
        gain_grad = to_all(part, ("xh", "core"), XH * CORE)
        gain_grad = gain_grad.reshape(XH, CORE, Z, 128).transpose(2, 0, 1, 3)

    with jax.named_scope("values"):
        scaled_weight = (weight_z.astype(f32) * gain_class[:, :, None]).astype(bf16)
        scaled_weight = pair(scaled_weight, swap(scaled_weight, "xh"), xh, 1)
        scaled_weight = pair(scaled_weight, swap(scaled_weight, "core"), core, 2)
        values = jnp.dot(
            activations, scaled_weight.reshape(8192, 128), preferred_element_type=f32
        )
        values = (values * inverse).astype(bf16)

    with jax.named_scope("outer_update"):
        delta = (global_slab - local_slab[0].astype(f32)).astype(bf16)
        average = jnp.sum(to_all(delta, "island", 8).astype(f32), axis=0) / 8
        new_momentum = 0.9 * momentum + average
        new_global = global_slab - 0.7 * (average + 0.9 * new_momentum)

    fsdp_index = (lax.axis_index("z") * XH + xh) * CORE + core
    gain_own = lax.dynamic_index_in_dim(norm_gain.reshape(64, 128), fsdp_index, 0, False)
    weight_grad = grad_own * gain_own[:, None]
    return (values, weight_grad[None], gain_grad.reshape(1, 8192), new_global, new_momentum)


def solution(mesh):
    mesh = Mesh(np.asarray(mesh.devices).reshape(8, Z, XH, CORE), ("island",) + FSDP)
    every = ("island",) + FSDP
    placed = (
        P(every, None),
        P(every, None),
        P("island", None),
        P("island", FSDP, None),
        P(None, FSDP),
        P("island", None, FSDP),
        P(None, FSDP),
    )
    return jax.shard_map(
        shards,
        mesh=mesh,
        in_specs=placed,
        out_specs=(
            P(every, None),
            P("island", FSDP, None),
            P("island", None),
            P(None, FSDP),
            P(None, FSDP),
        ),
        check_vma=False,
    )
```

```python
import functools

import jax
import jax.numpy as jnp
import numpy as np
from jax import lax
from jax.experimental import pallas as pl
from jax.experimental.pallas import tpu as pltpu
from jax.sharding import Mesh, PartitionSpec as P

FSDP = ("zh", "zl", "xh", "core")
QUAD = ("zl", "xh")
ZL = XH = CORE = 2
B = 128
f32, bf16 = jnp.float32, jnp.bfloat16
SMEM = pl.BlockSpec(memory_space=pltpu.SMEM)
VMEM = pl.BlockSpec(memory_space=pltpu.VMEM)
LIMIT = 60 * 2**20
SMALL = 20 * 2**20


def swap(value, axis, flip=1, size=2):
    return lax.ppermute(value, axis, [(i, i ^ flip) for i in range(size)])


def to_all(value, axis, size):
    return lax.all_to_all(jnp.broadcast_to(value[None], (size,) + value.shape), axis, 0, 0)


def whole(*shape):
    return pl.BlockSpec(shape, lambda *_: (0,) * len(shape))


def project_kernel(rows, place, x, cot, keep, send, inverse, scaled):
    tokens, width = x.shape
    for i in range(0, tokens, rows):
        total = jnp.zeros((rows, B), f32)
        for c in range(0, width, B):
            block = x[pl.ds(i, rows), pl.ds(c, B)].astype(f32)
            total += block * block
        mean = jnp.sum(total, axis=1, keepdims=True) * (1 / width)
        unit = lax.rsqrt(mean + 1e-05)
        inverse[pl.ds(i, rows), :] = unit
        scaled[pl.ds(i, rows), :] = cot[pl.ds(i, rows), :].astype(f32) * unit
    left = scaled[...].T.astype(bf16)
    core = place[0]
    for k in range(width // (CORE * B)):
        both = jnp.dot(left, x[:, pl.ds(k * CORE * B, CORE * B)], preferred_element_type=f32)
        both = both.astype(bf16)
        first, second = both[:, :B], both[:, B:]
        at, z = k % (ZL * XH), k // (ZL * XH)
        keep[at, z] = jnp.where(core == 0, first, second)
        send[at, z] = jnp.where(core == 0, second, first)


def project(place, activations, cotangent):
    tokens, width = activations.shape
    rows = 32
    half = jax.ShapeDtypeStruct((ZL * XH, width // (ZL * XH * CORE * B), B, B), bf16)
    return pl.pallas_call(
        functools.partial(project_kernel, rows),
        out_shape=(half, half, jax.ShapeDtypeStruct((tokens, 1), f32)),
        in_specs=[SMEM, VMEM, VMEM],
        out_specs=[VMEM] * 3,
        scratch_shapes=[
            pltpu.VMEM((tokens, B), f32),
        ],
        compiler_params=pltpu.CompilerParams(vmem_limit_bytes=SMALL),
        cost_estimate=pl.CostEstimate(
            flops=2 * tokens * width * B, bytes_accessed=3 * tokens * width, transcendentals=0
        ),
        name="project",
    )(place, activations, cotangent)


def relative(i, quad):
    low, high = quad % 2, quad // 2
    return (1 - high if i // 2 else high) * 2 + (1 - low if i % 2 else low)


def merge_kernel(place, keep, core_part, one, two, three, own):
    for i, out in enumerate((own, one, two, three)):
        at = relative(i, place[1])
        for z in range(keep.shape[1]):
            total = keep[at, z].astype(f32) + core_part[at, z].astype(f32)
            out[z] = total.astype(out.dtype)


def merge(place, keep, core_part):
    quad, z = keep.shape[:2]
    block = jax.ShapeDtypeStruct((z, B, B), bf16)
    return pl.pallas_call(
        merge_kernel,
        grid=(1,),
        out_shape=(block,) * 3 + (jax.ShapeDtypeStruct((z, B, B), f32),),
        in_specs=[SMEM] + [whole(*keep.shape)] * 2,
        out_specs=[whole(z, B, B)] * 4,
        compiler_params=pltpu.CompilerParams(vmem_limit_bytes=SMALL),
        cost_estimate=pl.CostEstimate(
            flops=quad * z * B * B, bytes_accessed=7 * quad * z * B * B, transcendentals=0
        ),
        name="merge",
    )(place, keep, core_part)


def combine_kernel(place, own, one, two, three, weight, out, gain):
    depth = own.shape[0]
    zl = place[1] // XH
    for z in range(depth):
        total = own[z] + one[z].astype(f32) + two[z].astype(f32) + three[z].astype(f32)
        out[z, pl.ds(0, B), :] = total.astype(bf16)
        terms = total * weight[ZL * z + zl].astype(f32).T
        gain[pl.ds(z, 1), :] = jnp.sum(terms, axis=0, keepdims=True)
    high = gain[...].astype(bf16)
    low = (gain[...] - high.astype(f32)).astype(bf16)
    terms = jnp.concatenate([high.astype(f32), low.astype(f32)], axis=0).astype(bf16)
    for z in range(depth):
        out[z, pl.ds(B, 2 * depth), :] = terms


def combine(place, own, parts, weight):
    z = own.shape[0]
    return pl.pallas_call(
        combine_kernel,
        grid=(1,),
        out_shape=jax.ShapeDtypeStruct((z, B + 2 * z, B), bf16),
        in_specs=[SMEM] + [whole(z, B, B)] * 4 + [whole(ZL * z, B, B)],
        out_specs=whole(z, B + 2 * z, B),
        scratch_shapes=[pltpu.VMEM((z, B), f32)],
        compiler_params=pltpu.CompilerParams(vmem_limit_bytes=SMALL),
        cost_estimate=pl.CostEstimate(
            flops=6 * z * B * B, bytes_accessed=14 * z * B * B, transcendentals=0
        ),
        name="combine",
    )(place, own, *parts, weight)


def values_kernel(place, x, inverse, gain, w00, w01, w10, w11, out):
    core = place[0]
    same = place[1] % XH == 0
    column = gain[...].T
    total = jnp.zeros(out.shape, f32)
    for k in range(x.shape[1] // (CORE * B)):
        xh, z = k % XH, k // XH
        near = same if xh == 0 else jnp.logical_not(same)
        here = jnp.where(near, w00[z].astype(f32), w01[z].astype(f32))
        there = jnp.where(near, w10[z].astype(f32), w11[z].astype(f32))
        first = jnp.where(core == 0, here, there) * column[:, 2 * k : 2 * k + 1]
        second = jnp.where(core == 0, there, here) * column[:, 2 * k + 1 : 2 * k + 2]
        weight = jnp.concatenate([first, second], axis=0).astype(bf16)
        columns = pl.ds(k * CORE * B, CORE * B)
        total += jnp.dot(x[:, columns], weight, preferred_element_type=f32)
    out[...] = (total * inverse[...]).astype(bf16)


def project_forward(place, activations, inverse, gain, pieces):
    tokens, width = activations.shape
    return pl.pallas_call(
        values_kernel,
        out_shape=jax.ShapeDtypeStruct((tokens, B), bf16),
        in_specs=[SMEM] + [VMEM] * 7,
        out_specs=VMEM,
        compiler_params=pltpu.CompilerParams(vmem_limit_bytes=SMALL),
        cost_estimate=pl.CostEstimate(
            flops=2 * tokens * width * B, bytes_accessed=3 * tokens * width, transcendentals=0
        ),
        name="project_forward",
    )(place, activations, inverse, gain.reshape(-1, B), *pieces)


def sum_over_islands(delta, islands, flips):
    for flip in [f for f in flips if f < islands]:
        delta = delta + swap(delta, "island", flip, islands)
    return delta


def shards(activations, cotangent, norm_gain, weight, global_slab, local_slab, momentum):
    quad, core = lax.axis_index(QUAD), lax.axis_index("core")
    depth, islands = lax.axis_size("zh"), lax.axis_size("island")
    place = jnp.stack([core, quad]).astype(jnp.int32)

    with jax.named_scope("weight_over_z"):
        weight_z = to_all(weight[0], ("zh", "zl"), depth * ZL)

    with jax.named_scope("projection_grad"):
        keep, send, inverse = project(place, activations, cotangent)
        core_part = swap(send, "core")
        *sent, own = merge(place, keep, core_part)
        parts = [swap(part, QUAD, i, 4) for i, part in zip((1, 2, 3), sent)]

    with jax.named_scope("average_over_islands"):
        local, own = lax.optimization_barrier((local_slab, own))
        delta = (global_slab - local[0].astype(f32)).astype(bf16)
        average = sum_over_islands(delta.astype(f32), islands, (1, 3))

    with jax.named_scope("projection_grad"):
        combined = combine(place, own, parts, weight_z)
        combined, average = lax.optimization_barrier((combined, average))
        chunks = lax.all_to_all(combined, "zh", 0, 0)

    with jax.named_scope("values"):
        w01 = swap(weight_z, "xh")
        pieces = (weight_z, w01, swap(weight_z, "core"), swap(w01, "core"))
        values = project_forward(place, activations, inverse, norm_gain, pieces)

    with jax.named_scope("gain_grad"):
        chunks, *rest = lax.optimization_barrier((chunks, pieces[2], pieces[3]))
        gain_grad = jnp.sum(chunks[:, B:].astype(f32), axis=0)
        gain_grad = gain_grad[:depth] + gain_grad[depth:]
        gain_grad = to_all(gain_grad, QUAD + ("core",), ZL * XH * CORE)
        gain_grad = gain_grad.transpose(1, 0, 2)

    with jax.named_scope("weight_grad"):
        row = (lax.axis_index("zh") * ZL * XH + quad) * CORE + core
        gain_own = lax.dynamic_index_in_dim(norm_gain.reshape(-1, B), row, 0, True)
        weight_grad = (jnp.sum(chunks[:, :B].astype(f32), axis=0) * gain_own).T

    with jax.named_scope("outer_update"):
        average = sum_over_islands(average, islands, (4,)) / islands
        new_momentum = 0.9 * momentum + average
        new_global = global_slab - 0.7 * (average + 0.9 * new_momentum)

    return (values, weight_grad[None], gain_grad.reshape(1, -1), new_global, new_momentum)


def solution(mesh):
    islands, fsdp = mesh.shape["island"], mesh.shape["fsdp"]
    grid = np.asarray(mesh.devices).reshape(islands, fsdp // (ZL * XH * CORE), ZL, XH, CORE)
    every = ("island",) + FSDP
    return jax.shard_map(
        shards,
        mesh=Mesh(grid, every),
        in_specs=(
            P(every, None),
            P(every, None),
            P("island", None),
            P("island", FSDP, None),
            P(None, FSDP),
            P("island", None, FSDP),
            P(None, FSDP),
        ),
        out_specs=(
            P(every, None),
            P("island", FSDP, None),
            P("island", None),
            P(None, FSDP),
            P(None, FSDP),
        ),
        check_vma=False,
    )
```

```python
import functools

import jax
import jax.numpy as jnp
import numpy as np
from jax import lax
from jax.experimental import pallas as pl
from jax.experimental.pallas import tpu as pltpu
from jax.sharding import Mesh, PartitionSpec as P

FSDP = ("zh", "zl", "xh", "core")
QUAD = ("zl", "xh")
ZL = XH = CORE = 2
B = 128
f32, bf16 = jnp.float32, jnp.bfloat16
SMEM = pl.BlockSpec(memory_space=pltpu.SMEM)
VMEM = pl.BlockSpec(memory_space=pltpu.VMEM)
SMALL = 20 * 2**20


def swap(value, axis, flip=1, size=2):
    return lax.ppermute(value, axis, [(i, i ^ flip) for i in range(size)])


def to_all(value, axis, size):
    return lax.all_to_all(jnp.broadcast_to(value[None], (size,) + value.shape), axis, 0, 0)


def whole(*shape):
    return pl.BlockSpec(shape, lambda *_: (0,) * len(shape))


def spread_kernel(value, out):
    for i in range(out.shape[0]):
        out[i] = value[0]


def spread(value, size):
    return pl.pallas_call(
        spread_kernel,
        out_shape=jax.ShapeDtypeStruct((size,) + value.shape[1:], value.dtype),
        in_specs=[VMEM],
        out_specs=VMEM,
        compiler_params=pltpu.CompilerParams(vmem_limit_bytes=SMALL),
        name="spread",
    )(value)


def project_kernel(rows, place, x, cot, keep, send, inverse, scaled):
    tokens, width = x.shape
    for i in range(0, tokens, rows):
        total = jnp.zeros((rows, B), f32)
        for c in range(0, width, B):
            block = x[pl.ds(i, rows), pl.ds(c, B)].astype(f32)
            total += block * block
        mean = jnp.sum(total, axis=1, keepdims=True) * (1 / width)
        unit = lax.rsqrt(mean + 1e-05)
        inverse[pl.ds(i, rows), :] = unit
        scaled[pl.ds(i, rows), :] = cot[pl.ds(i, rows), :].astype(f32) * unit
    left = scaled[...].T.astype(bf16)
    core = place[0]
    for k in range(width // (CORE * B)):
        both = jnp.dot(left, x[:, pl.ds(k * CORE * B, CORE * B)], preferred_element_type=f32)
        both = both.astype(bf16)
        first, second = both[:, :B], both[:, B:]
        at, z = k % (ZL * XH), k // (ZL * XH)
        keep[at, z] = jnp.where(core == 0, first, second)
        send[at, z] = jnp.where(core == 0, second, first)


def project(place, activations, cotangent):
    tokens, width = activations.shape
    rows = 32
    half = jax.ShapeDtypeStruct((ZL * XH, width // (ZL * XH * CORE * B), B, B), bf16)
    return pl.pallas_call(
        functools.partial(project_kernel, rows),
        out_shape=(half, half, jax.ShapeDtypeStruct((tokens, 1), f32)),
        in_specs=[SMEM, VMEM, VMEM],
        out_specs=[VMEM] * 3,
        scratch_shapes=[
            pltpu.VMEM((tokens, B), f32),
        ],
        compiler_params=pltpu.CompilerParams(vmem_limit_bytes=SMALL),
        cost_estimate=pl.CostEstimate(
            flops=2 * tokens * width * B, bytes_accessed=3 * tokens * width, transcendentals=0
        ),
        name="project",
    )(place, activations, cotangent)


def relative(i, quad):
    low, high = quad % 2, quad // 2
    return (1 - high if i // 2 else high) * 2 + (1 - low if i % 2 else low)


def merge_kernel(place, keep, core_part, one, two, three, own):
    for i, out in enumerate((own, one, two, three)):
        at = relative(i, place[1])
        for z in range(keep.shape[1]):
            total = keep[at, z].astype(f32) + core_part[at, z].astype(f32)
            out[z] = total.astype(out.dtype)


def merge(place, keep, core_part):
    quad, z = keep.shape[:2]
    block = jax.ShapeDtypeStruct((z, B, B), bf16)
    return pl.pallas_call(
        merge_kernel,
        grid=(1,),
        out_shape=(block,) * 3 + (jax.ShapeDtypeStruct((z, B, B), f32),),
        in_specs=[SMEM] + [whole(*keep.shape)] * 2,
        out_specs=[whole(z, B, B)] * 4,
        compiler_params=pltpu.CompilerParams(vmem_limit_bytes=SMALL),
        cost_estimate=pl.CostEstimate(
            flops=quad * z * B * B, bytes_accessed=7 * quad * z * B * B, transcendentals=0
        ),
        name="merge",
    )(place, keep, core_part)


def combine_kernel(place, own, one, two, three, weight, out, gain):
    depth = own.shape[0]
    zl = place[1] // XH
    for z in range(depth):
        total = own[z] + one[z].astype(f32) + two[z].astype(f32) + three[z].astype(f32)
        out[z, pl.ds(0, B), :] = total.astype(bf16)
        terms = total * weight[ZL * z + zl].astype(f32).T
        gain[pl.ds(z, 1), :] = jnp.sum(terms, axis=0, keepdims=True)
    high = gain[...].astype(bf16)
    low = (gain[...] - high.astype(f32)).astype(bf16)
    terms = jnp.concatenate([high.astype(f32), low.astype(f32)], axis=0).astype(bf16)
    for z in range(depth):
        out[z, pl.ds(B, 2 * depth), :] = terms


def combine(place, own, parts, weight):
    z = own.shape[0]
    return pl.pallas_call(
        combine_kernel,
        grid=(1,),
        out_shape=jax.ShapeDtypeStruct((z, B + 2 * z, B), bf16),
        in_specs=[SMEM] + [whole(z, B, B)] * 4 + [whole(ZL * z, B, B)],
        out_specs=whole(z, B + 2 * z, B),
        scratch_shapes=[pltpu.VMEM((z, B), f32)],
        compiler_params=pltpu.CompilerParams(vmem_limit_bytes=SMALL),
        cost_estimate=pl.CostEstimate(
            flops=6 * z * B * B, bytes_accessed=14 * z * B * B, transcendentals=0
        ),
        name="combine",
    )(place, own, *parts, weight)


def values_kernel(place, x, inverse, gain, w00, w01, w10, w11, out):
    core = place[0]
    same = place[1] % XH == 0
    column = gain[...].T
    total = jnp.zeros(out.shape, f32)
    for k in range(x.shape[1] // (CORE * B)):
        xh, z = k % XH, k // XH
        near = same if xh == 0 else jnp.logical_not(same)
        here = jnp.where(near, w00[z].astype(f32), w01[z].astype(f32))
        there = jnp.where(near, w10[z].astype(f32), w11[z].astype(f32))
        first = jnp.where(core == 0, here, there) * column[:, 2 * k : 2 * k + 1]
        second = jnp.where(core == 0, there, here) * column[:, 2 * k + 1 : 2 * k + 2]
        weight = jnp.concatenate([first, second], axis=0).astype(bf16)
        columns = pl.ds(k * CORE * B, CORE * B)
        total += jnp.dot(x[:, columns], weight, preferred_element_type=f32)
    out[...] = (total * inverse[...]).astype(bf16)


def project_forward(place, activations, inverse, gain, pieces):
    tokens, width = activations.shape
    return pl.pallas_call(
        values_kernel,
        out_shape=jax.ShapeDtypeStruct((tokens, B), bf16),
        in_specs=[SMEM] + [VMEM] * 7,
        out_specs=VMEM,
        compiler_params=pltpu.CompilerParams(vmem_limit_bytes=SMALL),
        cost_estimate=pl.CostEstimate(
            flops=2 * tokens * width * B, bytes_accessed=3 * tokens * width, transcendentals=0
        ),
        name="project_forward",
    )(place, activations, inverse, gain.reshape(-1, B), *pieces)


def shards(activations, cotangent, norm_gain, weight, global_slab, local_slab, momentum):
    quad, core = lax.axis_index(QUAD), lax.axis_index("core")
    depth, islands = lax.axis_size("zh"), lax.axis_size("island")
    place = jnp.stack([core, quad]).astype(jnp.int32)

    with jax.named_scope("weight_over_z"):
        weight_z = lax.all_to_all(spread(weight, depth * ZL), ("zh", "zl"), 0, 0)

    with jax.named_scope("projection_grad"):
        keep, send, inverse = project(place, activations, cotangent)
        core_part = swap(send, "core")
        *sent, own = merge(place, keep, core_part)
        parts = [swap(part, QUAD, i, 4) for i, part in zip((1, 2, 3), sent)]

    with jax.named_scope("deltas_over_islands"):
        local = lax.optimization_barrier((local_slab, own))[0]
        delta = (global_slab - local[0].astype(f32)).astype(bf16).astype(f32)
        delta = delta + swap(delta, "island", 1, islands)
        delta_y = swap(delta, "island", 3, islands)

    with jax.named_scope("projection_grad"):
        combined = combine(place, own, parts, weight_z)
        combined, delta_y = lax.optimization_barrier((combined, delta_y))
        chunks = lax.all_to_all(combined, "zh", 0, 0)

    with jax.named_scope("values"):
        later = lax.optimization_barrier((weight_z, delta))[0]
        w01 = swap(later, "xh")
        pieces = (weight_z, w01, swap(weight_z, "core"), swap(w01, "core"))
        values = project_forward(place, activations, inverse, norm_gain, pieces)

    with jax.named_scope("deltas_over_islands"):
        delta = delta + delta_y
        delta_x = swap(delta, "island", 4, islands)

    with jax.named_scope("gain_grad"):
        chunks, values = lax.optimization_barrier((chunks, values))
        gain_grad = jnp.sum(chunks[:, B:].astype(f32), axis=0)
        gain_grad = gain_grad[:depth] + gain_grad[depth:]
        gain_grad = to_all(gain_grad, QUAD + ("core",), ZL * XH * CORE)
        gain_grad = gain_grad.transpose(1, 0, 2)

    with jax.named_scope("weight_grad"):
        row = (lax.axis_index("zh") * ZL * XH + quad) * CORE + core
        gain_own = lax.dynamic_index_in_dim(norm_gain.reshape(-1, B), row, 0, True)
        weight_grad = (jnp.sum(chunks[:, :B].astype(f32), axis=0) * gain_own).T

    with jax.named_scope("outer_update"):
        delta_x = lax.optimization_barrier((delta_x, chunks))[0]
        average = (delta + delta_x) / islands
        new_momentum = 0.9 * momentum + average
        new_global = global_slab - 0.7 * (average + 0.9 * new_momentum)

    return (values, weight_grad[None], gain_grad.reshape(1, -1), new_global, new_momentum)


def solution(mesh):
    islands, fsdp = mesh.shape["island"], mesh.shape["fsdp"]
    grid = np.asarray(mesh.devices).reshape(islands, fsdp // (ZL * XH * CORE), ZL, XH, CORE)
    every = ("island",) + FSDP
    return jax.shard_map(
        shards,
        mesh=Mesh(grid, every),
        in_specs=(
            P(every, None),
            P(every, None),
            P("island", None),
            P("island", FSDP, None),
            P(None, FSDP),
            P("island", None, FSDP),
            P(None, FSDP),
        ),
        out_specs=(
            P(every, None),
            P("island", FSDP, None),
            P("island", None),
            P(None, FSDP),
            P(None, FSDP),
        ),
        check_vma=False,
    )
```

```python
import functools

import jax
import jax.numpy as jnp
import numpy as np
from jax import lax
from jax.experimental import pallas as pl
from jax.experimental.pallas import tpu as pltpu
from jax.sharding import Mesh, PartitionSpec as P

FSDP = ("zh", "zl", "xh", "core")
QUAD = ("zl", "xh")
ZL = XH = CORE = 2
B = 128
f32, bf16 = jnp.float32, jnp.bfloat16
VMEM = pl.BlockSpec(memory_space=pltpu.VMEM)
SMALL = 20 * 2**20


def swap(value, axis, flip=1, size=2):
    return lax.ppermute(value, axis, [(i, i ^ flip) for i in range(size)])


def to_all(value, axis, size):
    return lax.all_to_all(jnp.broadcast_to(value[None], (size,) + value.shape), axis, 0, 0)


def whole(*shape):
    return pl.BlockSpec(shape, lambda *_: (0,) * len(shape))


def spread_kernel(value, out):
    for i in range(out.shape[0]):
        out[i] = value[0]


def spread(value, size):
    return pl.pallas_call(
        spread_kernel,
        out_shape=jax.ShapeDtypeStruct((size,) + value.shape[1:], value.dtype),
        in_specs=[VMEM],
        out_specs=VMEM,
        compiler_params=pltpu.CompilerParams(vmem_limit_bytes=SMALL),
        name="spread",
    )(value)


def project_kernel(rows, x, cot, keep, send, inverse, scaled):
    tokens, width = x.shape
    for i in range(0, tokens, rows):
        total = jnp.zeros((rows, B), f32)
        for c in range(0, width, B):
            block = x[pl.ds(i, rows), pl.ds(c, B)].astype(f32)
            total += block * block
        mean = jnp.sum(total, axis=1, keepdims=True) * (1 / width)
        unit = lax.rsqrt(mean + 1e-05)
        inverse[pl.ds(i, rows), :] = unit
        scaled[pl.ds(i, rows), :] = cot[pl.ds(i, rows), :].astype(f32) * unit
    left = scaled[...].T.astype(bf16)
    core = lax.axis_index("core")
    for k in range(width // (CORE * B)):
        both = jnp.dot(left, x[:, pl.ds(k * CORE * B, CORE * B)], preferred_element_type=f32)
        both = both.astype(bf16)
        first, second = both[:, :B], both[:, B:]
        at, z = k % (ZL * XH), k // (ZL * XH)
        keep[at, z] = jnp.where(core == 0, first, second)
        send[at, z] = jnp.where(core == 0, second, first)


def project(activations, cotangent):
    tokens, width = activations.shape
    rows = 32
    half = jax.ShapeDtypeStruct((ZL * XH, width // (ZL * XH * CORE * B), B, B), bf16)
    return pl.pallas_call(
        functools.partial(project_kernel, rows),
        out_shape=(half, half, jax.ShapeDtypeStruct((tokens, 1), f32)),
        in_specs=[VMEM, VMEM],
        out_specs=[VMEM] * 3,
        scratch_shapes=[
            pltpu.VMEM((tokens, B), f32),
        ],
        compiler_params=pltpu.CompilerParams(vmem_limit_bytes=SMALL),
        cost_estimate=pl.CostEstimate(
            flops=2 * tokens * width * B, bytes_accessed=3 * tokens * width, transcendentals=0
        ),
        name="project",
    )(activations, cotangent)


def relative(i, quad):
    low, high = quad % 2, quad // 2
    return (1 - high if i // 2 else high) * 2 + (1 - low if i % 2 else low)


def merge_kernel(keep, core_part, both, xh, zl, own):
    for i, out in ((0, own), (3, both), (1, xh), (2, zl)):
        at = relative(i, lax.axis_index(QUAD))
        for z in range(keep.shape[1]):
            total = keep[at, z].astype(f32) + core_part[at, z].astype(f32)
            out[z] = total.astype(out.dtype)


def merge(keep, core_part):
    quad, z = keep.shape[:2]
    block = jax.ShapeDtypeStruct((z, B, B), bf16)
    return pl.pallas_call(
        merge_kernel,
        grid=(1,),
        out_shape=(block,) * 3 + (jax.ShapeDtypeStruct((z, B, B), f32),),
        in_specs=[whole(*keep.shape)] * 2,
        out_specs=[whole(z, B, B)] * 4,
        compiler_params=pltpu.CompilerParams(vmem_limit_bytes=SMALL),
        cost_estimate=pl.CostEstimate(
            flops=quad * z * B * B, bytes_accessed=7 * quad * z * B * B, transcendentals=0
        ),
        name="merge",
    )(keep, core_part)


def combine_kernel(own, one, two, three, weight, out, gain):
    depth = own.shape[0]
    zl = lax.axis_index(QUAD) // XH
    for z in range(depth):
        total = own[z] + one[z].astype(f32) + two[z].astype(f32) + three[z].astype(f32)
        out[z, pl.ds(0, B), :] = total.astype(bf16)
        terms = total * weight[ZL * z + zl].astype(f32).T
        gain[pl.ds(z, 1), :] = jnp.sum(terms, axis=0, keepdims=True)
    high = gain[...].astype(bf16)
    low = (gain[...] - high.astype(f32)).astype(bf16)
    terms = jnp.concatenate([high.astype(f32), low.astype(f32)], axis=0).astype(bf16)
    for z in range(depth):
        out[z, pl.ds(B, 2 * depth), :] = terms


def combine(own, parts, weight):
    z = own.shape[0]
    return pl.pallas_call(
        combine_kernel,
        grid=(1,),
        out_shape=jax.ShapeDtypeStruct((z, B + 2 * z, B), bf16),
        in_specs=[whole(z, B, B)] * 4 + [whole(ZL * z, B, B)],
        out_specs=whole(z, B + 2 * z, B),
        scratch_shapes=[pltpu.VMEM((z, B), f32)],
        compiler_params=pltpu.CompilerParams(vmem_limit_bytes=SMALL),
        cost_estimate=pl.CostEstimate(
            flops=6 * z * B * B, bytes_accessed=14 * z * B * B, transcendentals=0
        ),
        name="combine",
    )(own, *parts, weight)


def values_kernel(x, inverse, gain, w00, w01, w10, w11, out):
    core = lax.axis_index("core")
    same = lax.axis_index(QUAD) % XH == 0
    column = gain[...].T
    total = jnp.zeros(out.shape, f32)
    for k in range(x.shape[1] // (CORE * B)):
        xh, z = k % XH, k // XH
        near = same if xh == 0 else jnp.logical_not(same)
        here = jnp.where(near, w00[z].astype(f32), w01[z].astype(f32))
        there = jnp.where(near, w10[z].astype(f32), w11[z].astype(f32))
        first = jnp.where(core == 0, here, there) * column[:, 2 * k : 2 * k + 1]
        second = jnp.where(core == 0, there, here) * column[:, 2 * k + 1 : 2 * k + 2]
        weight = jnp.concatenate([first, second], axis=0).astype(bf16)
        columns = pl.ds(k * CORE * B, CORE * B)
        total += jnp.dot(x[:, columns], weight, preferred_element_type=f32)
    out[...] = (total * inverse[...]).astype(bf16)


def project_forward(activations, inverse, gain, pieces):
    tokens, width = activations.shape
    return pl.pallas_call(
        values_kernel,
        out_shape=jax.ShapeDtypeStruct((tokens, B), bf16),
        in_specs=[VMEM] * 7,
        out_specs=VMEM,
        compiler_params=pltpu.CompilerParams(vmem_limit_bytes=SMALL),
        cost_estimate=pl.CostEstimate(
            flops=2 * tokens * width * B, bytes_accessed=3 * tokens * width, transcendentals=0
        ),
        name="project_forward",
    )(activations, inverse, gain.reshape(-1, B), *pieces)


def shards(activations, cotangent, norm_gain, weight, global_slab, local_slab, momentum):
    quad, core = lax.axis_index(QUAD), lax.axis_index("core")
    depth, islands = lax.axis_size("zh"), lax.axis_size("island")

    with jax.named_scope("weight_over_z"):
        weight_z = lax.all_to_all(spread(weight, depth * ZL), ("zh", "zl"), 0, 0)

    with jax.named_scope("projection_grad"):
        keep, send, inverse = project(activations, cotangent)
        core_part = swap(send, "core")
        *sent, own = merge(keep, core_part)
        parts = [swap(part, QUAD, i, 4) for i, part in zip((3, 1, 2), sent)]

    with jax.named_scope("deltas_over_islands"):
        local = lax.optimization_barrier((local_slab, own))[0]
        delta = (global_slab - local[0].astype(f32)).astype(bf16).astype(f32)
        delta = delta + swap(delta, "island", 1, islands)
        delta_y = swap(delta, "island", 3, islands)

    with jax.named_scope("projection_grad"):
        combined = combine(own, parts, weight_z)
        combined, delta_y = lax.optimization_barrier((combined, delta_y))
        chunks = lax.all_to_all(combined, "zh", 0, 0)

    with jax.named_scope("values"):
        later = lax.optimization_barrier((weight_z, delta))[0]
        w01 = swap(later, "xh")
        pieces = (weight_z, w01, swap(weight_z, "core"), swap(w01, "core"))
        values = project_forward(activations, inverse, norm_gain, pieces)

    with jax.named_scope("deltas_over_islands"):
        delta = delta + delta_y
        delta_x = swap(delta, "island", 4, islands)

    with jax.named_scope("gain_grad"):
        chunks, values = lax.optimization_barrier((chunks, values))
        gain_grad = jnp.sum(chunks[:, B:].astype(f32), axis=0)
        gain_grad = gain_grad[:depth] + gain_grad[depth:]
        gain_grad = to_all(gain_grad, QUAD + ("core",), ZL * XH * CORE)
        gain_grad = gain_grad.transpose(1, 0, 2)

    with jax.named_scope("weight_grad"):
        row = (lax.axis_index("zh") * ZL * XH + quad) * CORE + core
        gain_own = lax.dynamic_index_in_dim(norm_gain.reshape(-1, B), row, 0, True)
        weight_grad = (jnp.sum(chunks[:, :B].astype(f32), axis=0) * gain_own).T

    with jax.named_scope("outer_update"):
        delta_x = lax.optimization_barrier((delta_x, chunks))[0]
        average = (delta + delta_x) / islands
        new_momentum = 0.9 * momentum + average
        new_global = global_slab - 0.7 * (average + 0.9 * new_momentum)

    return (values, weight_grad[None], gain_grad.reshape(1, -1), new_global, new_momentum)


def solution(mesh):
    islands, fsdp = mesh.shape["island"], mesh.shape["fsdp"]
    grid = np.asarray(mesh.devices).reshape(islands, fsdp // (ZL * XH * CORE), ZL, XH, CORE)
    every = ("island",) + FSDP
    return jax.shard_map(
        shards,
        mesh=Mesh(grid, every),
        in_specs=(
            P(every, None),
            P(every, None),
            P("island", None),
            P("island", FSDP, None),
            P(None, FSDP),
            P("island", None, FSDP),
            P(None, FSDP),
        ),
        out_specs=(
            P(every, None),
            P("island", FSDP, None),
            P("island", None),
            P(None, FSDP),
            P(None, FSDP),
        ),
        check_vma=False,
    )
```

```python
import functools

import jax
import jax.numpy as jnp
import numpy as np
from jax import lax
from jax.experimental import pallas as pl
from jax.experimental.pallas import tpu as pltpu
from jax.sharding import Mesh, PartitionSpec as P

FSDP = ("zh", "zl", "xh", "core")
QUAD = ("zl", "xh")
ZL = XH = CORE = 2
B = 128
f32, bf16 = jnp.float32, jnp.bfloat16
VMEM = pl.BlockSpec(memory_space=pltpu.VMEM)
SMALL = 20 * 2**20
LIMIT = 60 * 2**20


def swap(value, axis, flip=1, size=2):
    return lax.ppermute(value, axis, [(i, i ^ flip) for i in range(size)])


def to_all(value, axis, size):
    return lax.all_to_all(jnp.broadcast_to(value[None], (size,) + value.shape), axis, 0, 0)


def whole(*shape):
    return pl.BlockSpec(shape, lambda *_: (0,) * len(shape))


def spread_kernel(value, out, sems):
    copies = [
        pltpu.make_async_copy(value.at[0], out.at[i], sems.at[i]) for i in range(out.shape[0])
    ]
    for copy in copies:
        copy.start()
    for copy in copies:
        copy.wait()


def spread(value, size):
    return pl.pallas_call(
        spread_kernel,
        out_shape=jax.ShapeDtypeStruct((size,) + value.shape[1:], value.dtype),
        in_specs=[pl.BlockSpec(memory_space=pl.ANY)],
        out_specs=pl.BlockSpec(memory_space=pl.ANY),
        scratch_shapes=[pltpu.SemaphoreType.DMA((size,))],
        compiler_params=pltpu.CompilerParams(vmem_limit_bytes=LIMIT),
        name="spread",
    )(value)


def project_kernel(rows, x, cot, keep, send, inverse, scaled):
    tokens, width = x.shape
    for i in range(0, tokens, rows):
        total = jnp.zeros((rows, B), f32)
        for c in range(0, width, B):
            block = x[pl.ds(i, rows), pl.ds(c, B)].astype(f32)
            total += block * block
        mean = jnp.sum(total, axis=1, keepdims=True) * (1 / width)
        unit = lax.rsqrt(mean + 1e-05)
        inverse[pl.ds(i, rows), :] = unit
        scaled[pl.ds(i, rows), :] = cot[pl.ds(i, rows), :].astype(f32) * unit
    left = scaled[...].T.astype(bf16)
    core = lax.axis_index("core")
    for k in range(width // (CORE * B)):
        both = jnp.dot(left, x[:, pl.ds(k * CORE * B, CORE * B)], preferred_element_type=f32)
        both = both.astype(bf16)
        first, second = both[:, :B], both[:, B:]
        at, z = k % (ZL * XH), k // (ZL * XH)
        keep[at, z] = jnp.where(core == 0, first, second)
        send[at, z] = jnp.where(core == 0, second, first)


def project(activations, cotangent):
    tokens, width = activations.shape
    rows = 32
    half = jax.ShapeDtypeStruct((ZL * XH, width // (ZL * XH * CORE * B), B, B), bf16)
    return pl.pallas_call(
        functools.partial(project_kernel, rows),
        out_shape=(half, half, jax.ShapeDtypeStruct((tokens, 1), f32)),
        in_specs=[VMEM, VMEM],
        out_specs=[VMEM] * 3,
        scratch_shapes=[
            pltpu.VMEM((tokens, B), f32),
        ],
        compiler_params=pltpu.CompilerParams(vmem_limit_bytes=SMALL),
        cost_estimate=pl.CostEstimate(
            flops=2 * tokens * width * B, bytes_accessed=3 * tokens * width, transcendentals=0
        ),
        name="project",
    )(activations, cotangent)


def relative(i, quad):
    low, high = quad % 2, quad // 2
    return (1 - high if i // 2 else high) * 2 + (1 - low if i % 2 else low)


def merge_kernel(keep, core_part, both, xh, zl, own):
    for i, out in ((0, own), (3, both), (1, xh), (2, zl)):
        at = relative(i, lax.axis_index(QUAD))
        for z in range(keep.shape[1]):
            total = keep[at, z].astype(f32) + core_part[at, z].astype(f32)
            out[z] = total.astype(out.dtype)


def merge(keep, core_part):
    quad, z = keep.shape[:2]
    block = jax.ShapeDtypeStruct((z, B, B), bf16)
    return pl.pallas_call(
        merge_kernel,
        grid=(1,),
        out_shape=(block,) * 3 + (jax.ShapeDtypeStruct((z, B, B), f32),),
        in_specs=[whole(*keep.shape)] * 2,
        out_specs=[whole(z, B, B)] * 4,
        compiler_params=pltpu.CompilerParams(vmem_limit_bytes=SMALL),
        cost_estimate=pl.CostEstimate(
            flops=quad * z * B * B, bytes_accessed=7 * quad * z * B * B, transcendentals=0
        ),
        name="merge",
    )(keep, core_part)


def combine_kernel(own, one, two, three, weight, out, gain):
    depth = own.shape[0]
    zl = lax.axis_index(QUAD) // XH
    for z in range(depth):
        total = own[z] + one[z].astype(f32) + two[z].astype(f32) + three[z].astype(f32)
        out[z, pl.ds(0, B), :] = total.astype(bf16)
        terms = total * weight[ZL * z + zl].astype(f32).T
        gain[pl.ds(z, 1), :] = jnp.sum(terms, axis=0, keepdims=True)
    high = gain[...].astype(bf16)
    low = (gain[...] - high.astype(f32)).astype(bf16)
    terms = jnp.concatenate([high.astype(f32), low.astype(f32)], axis=0).astype(bf16)
    for z in range(depth):
        out[z, pl.ds(B, 2 * depth), :] = terms


def combine(own, parts, weight):
    z = own.shape[0]
    return pl.pallas_call(
        combine_kernel,
        grid=(1,),
        out_shape=jax.ShapeDtypeStruct((z, B + 2 * z, B), bf16),
        in_specs=[whole(z, B, B)] * 4 + [whole(ZL * z, B, B)],
        out_specs=whole(z, B + 2 * z, B),
        scratch_shapes=[pltpu.VMEM((z, B), f32)],
        compiler_params=pltpu.CompilerParams(vmem_limit_bytes=SMALL),
        cost_estimate=pl.CostEstimate(
            flops=6 * z * B * B, bytes_accessed=14 * z * B * B, transcendentals=0
        ),
        name="combine",
    )(own, *parts, weight)


def values_kernel(x, inverse, gain, w00, w01, w10, w11, out):
    core = lax.axis_index("core")
    same = lax.axis_index(QUAD) % XH == 0
    column = gain[...].T
    total = jnp.zeros(out.shape, f32)
    for k in range(x.shape[1] // (CORE * B)):
        xh, z = k % XH, k // XH
        near = same if xh == 0 else jnp.logical_not(same)
        here = jnp.where(near, w00[z].astype(f32), w01[z].astype(f32))
        there = jnp.where(near, w10[z].astype(f32), w11[z].astype(f32))
        first = jnp.where(core == 0, here, there) * column[:, 2 * k : 2 * k + 1]
        second = jnp.where(core == 0, there, here) * column[:, 2 * k + 1 : 2 * k + 2]
        weight = jnp.concatenate([first, second], axis=0).astype(bf16)
        columns = pl.ds(k * CORE * B, CORE * B)
        total += jnp.dot(x[:, columns], weight, preferred_element_type=f32)
    out[...] = (total * inverse[...]).astype(bf16)


def project_forward(activations, inverse, gain, pieces):
    tokens, width = activations.shape
    return pl.pallas_call(
        values_kernel,
        out_shape=jax.ShapeDtypeStruct((tokens, B), bf16),
        in_specs=[VMEM] * 7,
        out_specs=VMEM,
        compiler_params=pltpu.CompilerParams(vmem_limit_bytes=SMALL),
        cost_estimate=pl.CostEstimate(
            flops=2 * tokens * width * B, bytes_accessed=3 * tokens * width, transcendentals=0
        ),
        name="project_forward",
    )(activations, inverse, gain.reshape(-1, B), *pieces)


def shards(activations, cotangent, norm_gain, weight, global_slab, local_slab, momentum):
    quad, core = lax.axis_index(QUAD), lax.axis_index("core")
    depth, islands = lax.axis_size("zh"), lax.axis_size("island")

    with jax.named_scope("weight_over_z"):
        weight_z = lax.all_to_all(spread(weight, depth * ZL), ("zh", "zl"), 0, 0)

    with jax.named_scope("projection_grad"):
        keep, send, inverse = project(activations, cotangent)
        core_part = swap(send, "core")
        *sent, own = merge(keep, core_part)
        parts = [swap(part, QUAD, i, 4) for i, part in zip((3, 1, 2), sent)]

    with jax.named_scope("deltas_over_islands"):
        local = lax.optimization_barrier((local_slab, own))[0]
        delta = (global_slab - local[0].astype(f32)).astype(bf16).astype(f32)
        delta = delta + swap(delta, "island", 1, islands)
        delta_y = swap(delta, "island", 3, islands)

    with jax.named_scope("projection_grad"):
        combined = combine(own, parts, weight_z)
        combined, delta_y = lax.optimization_barrier((combined, delta_y))
        chunks = lax.all_to_all(combined, "zh", 0, 0)

    with jax.named_scope("values"):
        later = lax.optimization_barrier((weight_z, delta))[0]
        w01 = swap(later, "xh")
        pieces = (weight_z, w01, swap(weight_z, "core"), swap(w01, "core"))
        values = project_forward(activations, inverse, norm_gain, pieces)

    with jax.named_scope("deltas_over_islands"):
        delta = delta + delta_y
        delta_x = swap(delta, "island", 4, islands)

    with jax.named_scope("gain_grad"):
        chunks, values = lax.optimization_barrier((chunks, values))
        gain_grad = jnp.sum(chunks[:, B:].astype(f32), axis=0)
        gain_grad = gain_grad[:depth] + gain_grad[depth:]
        gain_grad = to_all(gain_grad, QUAD + ("core",), ZL * XH * CORE)
        gain_grad = gain_grad.transpose(1, 0, 2)

    with jax.named_scope("weight_grad"):
        row = (lax.axis_index("zh") * ZL * XH + quad) * CORE + core
        gain_own = lax.dynamic_index_in_dim(norm_gain.reshape(-1, B), row, 0, True)
        weight_grad = (jnp.sum(chunks[:, :B].astype(f32), axis=0) * gain_own).T

    with jax.named_scope("outer_update"):
        delta_x = lax.optimization_barrier((delta_x, chunks))[0]
        average = (delta + delta_x) / islands
        new_momentum = 0.9 * momentum + average
        new_global = global_slab - 0.7 * (average + 0.9 * new_momentum)

    return (values, weight_grad[None], gain_grad.reshape(1, -1), new_global, new_momentum)


def solution(mesh):
    islands, fsdp = mesh.shape["island"], mesh.shape["fsdp"]
    grid = np.asarray(mesh.devices).reshape(islands, fsdp // (ZL * XH * CORE), ZL, XH, CORE)
    every = ("island",) + FSDP
    return jax.shard_map(
        shards,
        mesh=Mesh(grid, every),
        in_specs=(
            P(every, None),
            P(every, None),
            P("island", None),
            P("island", FSDP, None),
            P(None, FSDP),
            P("island", None, FSDP),
            P(None, FSDP),
        ),
        out_specs=(
            P(every, None),
            P("island", FSDP, None),
            P("island", None),
            P(None, FSDP),
            P(None, FSDP),
        ),
        check_vma=False,
    )
```
